128 devices in a mesh: dom: 16 (over x, y), sub: 8 (over z, core).
Axes of the slice: x: 4, y: 4, z: 4, core: 2. Of those that a mesh axis runs over, the one named last changes fastest.
Arguments:
- basis: bfloat16 [1048576, 256], P(('dom', 'sub')), may hold values from -100 to 100
- block_part: int32 [8192], P(('dom', 'sub')), may hold values from 0 to 127, as said below
- block_slot: int32 [8192], P(('dom', 'sub')), may hold values from 0 to 127, as said below
- face_slots: int32 [512, 4], P(('dom', 'sub')), may hold values from 0 to 127, as said below
- neighbors: int32 [16384, 3], P(('dom', 'sub')), may hold values from 0 to 159, as said below
- jacobian: bfloat16 [16384, 3, 128, 128], P(('dom', 'sub')), may hold values from -2 to 6
Outputs:
- galerkin: float32 [256, 256], replicated
- lspg: float32 [256, 256], replicated
- applied: bfloat16 [2097152, 256], P(('dom', 'sub'))
The draws below stay inside these ranges and needn't reach their ends.
Inputs may be any that keep to these rules, and one draw needn't show every extreme that they name: `block_part`: each device's 64 blocks go to 64 different partitions, exactly 1 to each; a quarter of the partitions receive 128 blocks, a quarter 128 // 2, the others 128 // 4. The pairs (block_part, block_slot) are all different. `face_slots`: every entry names a slot of that partition which holds a block. `neighbors`: the first entry of a row is the row's own slot; entries of live slots name a live local slot or a halo entry.
All inputs are finite; a program needn't handle non-finite values.
Results may differ from the reference program's by a relative error of at most 0.0004.
Values may be sent and summed in bfloat16 or wider, within the bound.
A program may use at most 192 MiB of HBM per device.

```python
import math
import jax
import jax.numpy as jnp
from jax import lax

B = 128
K = 256
NNB = 3
H = 4
NB_DEV = 64
NPART = 128
PAIR = 1
CAP = 128
NBLK = 8192
ROWS = 1048576
N_DOM = 16
N_SUB = 8


def regroup_maps(key):
    base = jax.random.fold_in(key, 11)
    key_order, key_blocks, key_slots = jax.random.split(base, 3)
    quarter = NPART // 4
    pattern = jnp.concatenate([jnp.full((quarter,), NPART, jnp.int32), jnp.full((quarter,), NPART // 2, jnp.int32), jnp.full((NPART - 2 * quarter,), NPART // 4, jnp.int32)])
    unit_count = pattern[jax.random.permutation(key_order, NPART)]
    end_index = jnp.cumsum(unit_count).astype(jnp.int32)
    starts = end_index - unit_count
    per_source = NB_DEV // PAIR
    unit_ids = jnp.arange(NPART, dtype=jnp.int32)[:, None] + NPART * jnp.arange(per_source, dtype=jnp.int32)[None, :]
    column = jnp.sum((end_index[None, None, :] <= unit_ids[:, :, None]).astype(jnp.int32), axis=2)
    within = unit_ids - starts[column]
    entries = jax.vmap(lambda subkey: jax.random.permutation(subkey, NB_DEV))(jax.random.split(key_blocks, NPART)).astype(jnp.int32)
    unit_of = entries // PAIR
    member = entries % PAIR
    target = jnp.take_along_axis(column, unit_of, axis=1)
    order_rank = jnp.take_along_axis(within, unit_of, axis=1) * PAIR + member
    slot_perm = jax.vmap(lambda subkey: jax.random.permutation(subkey, CAP))(jax.random.split(key_slots, NPART)).astype(jnp.int32)
    slot_index = slot_perm[target, order_rank]
    return (target.reshape(-1).astype(jnp.int32), slot_index.reshape(-1).astype(jnp.int32), (unit_count * PAIR).astype(jnp.int32), slot_perm)


def draw_block_part(key, part):
    return regroup_maps(key)[0]


def draw_block_slot(key, part):
    return regroup_maps(key)[1]


def draw_face_slots(key, part):
    maps = regroup_maps(key)
    loads = maps[2]
    slot_perm = maps[3]
    picks = jax.random.randint(jax.random.fold_in(key, 23), (NPART, 4 * H), 0, loads[:, None])
    chosen = jnp.take_along_axis(slot_perm, picks.astype(jnp.int32), axis=1)
    return chosen.reshape(NPART * 4, H).astype(jnp.int32)


def draw_neighbors(key, part):
    maps = regroup_maps(key)
    loads = maps[2]
    slot_perm = maps[3]
    picks = jax.random.randint(jax.random.fold_in(key, 37), (NPART, CAP * (NNB - 1)), 0, loads[:, None] + 8 * H).astype(jnp.int32)
    local_pick = jnp.minimum(picks, loads[:, None] - 1)
    local_slot = jnp.take_along_axis(slot_perm, local_pick, axis=1)
    chosen = jnp.where(picks < loads[:, None], local_slot, CAP + picks - loads[:, None])
    chosen = chosen.reshape(NPART, CAP, NNB - 1)
    itself = jnp.broadcast_to(jnp.arange(CAP, dtype=jnp.int32)[None, :, None], (NPART, CAP, 1))
    return jnp.concatenate([itself, chosen], axis=2).reshape(NPART * CAP, NNB).astype(jnp.int32)


def draw_jacobian(key, part):
    shape = (NPART * CAP, NNB, B, B)
    key_noise, key_rows, key_diag = jax.random.split(jax.random.fold_in(key, 31), 3)
    partition = (jnp.arange(NPART * CAP, dtype=jnp.int32) // CAP).astype(jnp.float32)
    rising = 1.0 + 2.0 * partition / max(NPART - 1, 1)
    noise = jnp.clip(jax.random.normal(key_noise, shape, jnp.float32), -5.0, 5.0)
    row_scale = jnp.exp(jax.random.uniform(key_rows, (NPART * CAP, 1, B, 1), jnp.float32, math.log(0.7), math.log(1.4)))
    diag_scale = jax.random.uniform(key_diag, (NPART * CAP, 1, B), jnp.float32, 0.8, 1.2)
    off_part = noise * row_scale / math.sqrt(NNB * B)
    identity = (jnp.arange(B)[:, None] == jnp.arange(B)[None, :]).astype(jnp.float32)
    first = (jnp.arange(NNB) == 0).astype(jnp.float32)
    diag_part = rising[:, None, None, None] * first[None, :, None, None] * identity[None, None, :, :] * diag_scale[:, :, :, None]
    return (off_part + diag_part).astype(jnp.bfloat16)


def draw_basis(key, part):
    owner = regroup_maps(key)[0]
    key = jax.random.fold_in(key, 41)
    key_noise, key_rows = jax.random.split(key, 2)
    period = min(K, NPART)
    row_owner = jnp.repeat(owner % period, B, total_repeat_length=ROWS)
    column_mark = jnp.arange(K, dtype=jnp.int32) % period
    owned = (row_owner[:, None] == column_mark[None, :]).astype(jnp.float32)
    lift = 1.0 + 3.0 * owned
    row_scale = jnp.exp(jax.random.uniform(key_rows, (ROWS, 1), jnp.float32, math.log(0.4), math.log(4.0)))
    noise = jnp.clip(jax.random.normal(key_noise, (ROWS, K), jnp.float32), -5.0, 5.0)
    values = noise * row_scale * lift
    return jnp.clip(values, -100.0, 100.0).astype(jnp.bfloat16)


def setup_inputs(seed: int = 0) -> dict:
    seeds = jax.random.split(jax.random.key(seed), 7)
    basis = draw_basis(jax.random.fold_in(seeds[6], 71), 0)
    block_part = draw_block_part(jax.random.fold_in(seeds[6], 71), 0)
    block_slot = draw_block_slot(jax.random.fold_in(seeds[6], 71), 0)
    face_slots = draw_face_slots(jax.random.fold_in(seeds[6], 71), 0)
    neighbors = draw_neighbors(jax.random.fold_in(seeds[6], 71), 0)
    jacobian = draw_jacobian(jax.random.fold_in(seeds[6], 71), 0)
    return dict(basis=basis, block_part=block_part, block_slot=block_slot, face_slots=face_slots, neighbors=neighbors, jacobian=jacobian)


def reference(basis, block_part, block_slot, face_slots, neighbors, jacobian):
    blocks = basis.reshape(NBLK, B, K)
    target = (block_part * CAP + block_slot).astype(jnp.int32)
    table = jnp.zeros((NPART * CAP, B, K), jnp.bfloat16).at[target].set(blocks)
    live = jnp.zeros((NPART * CAP,), jnp.float32).at[target].set(1.0)
    partition = jnp.arange(NPART, dtype=jnp.int32)
    first_index = partition // N_SUB
    second_index = partition % N_SUB
    pieces = [partition[:, None] * CAP + jnp.arange(CAP, dtype=jnp.int32)[None, :]]
    grouped = face_slots.reshape(NPART, 4, H)
    sources_spec = [(-1, 0, 2), (-1, 0, 3), (1, 0, 0), (1, 0, 1), (0, -1, 1), (0, -1, 3), (0, 1, 0), (0, 1, 2)]
    for shift_dom, shift_sub, group in sources_spec:
        source = ((first_index + shift_dom) % N_DOM) * N_SUB + (second_index + shift_sub) % N_SUB
        pieces.append(source[:, None] * CAP + grouped[source, group, :])
    full_index = jnp.concatenate(pieces, axis=1).astype(jnp.int32)

    def per_partition(items):
        jac_part, near_part, index_part, live_part, table_part = items
        global_index = jnp.take(index_part, near_part, axis=0).astype(jnp.int32)
        gathered = table[global_index]
        product = jnp.einsum('snij,snjk->sik', jac_part.astype(jnp.float32), gathered.astype(jnp.float32))
        applied_part = (product * live_part[:, None, None]).astype(jnp.bfloat16)
        applied_wide = applied_part.astype(jnp.float32)
        galerkin_part = jnp.einsum('sbk,sbl->kl', table_part.astype(jnp.float32), applied_wide)
        lspg_part = jnp.einsum('sbk,sbl->kl', applied_wide, applied_wide)
        return applied_part, galerkin_part, lspg_part

    applied, galerkin_parts, lspg_parts = lax.map(per_partition, (
        jacobian.reshape(NPART, CAP, NNB, B, B),
        neighbors.reshape(NPART, CAP, NNB),
        full_index,
        live.reshape(NPART, CAP),
        table.reshape(NPART, CAP, B, K)))
    galerkin = jnp.sum(galerkin_parts, axis=0) / ROWS
    lspg = jnp.sum(lspg_parts, axis=0) / ROWS
    return galerkin, lspg, applied.reshape(NPART * CAP * B, K)
```

```python
import functools

import jax
import jax.numpy as jnp
from jax import lax
from jax.experimental import pallas as pl
from jax.experimental.pallas import tpu as pltpu
from jax.sharding import PartitionSpec as P

MESH = pl.DeviceIdType.MESH
BF16 = jnp.bfloat16
F32 = jnp.float32
I32 = jnp.int32

SLABS = ((48, 48, 32), (32, 48, 48))
ORDERS = ((0, 1, 2), (1, 2, 0), (2, 0, 1))
FACES = 4
GL_SLOTS = 4


def offsets(h):
    out, at = [], 0
    for rows in SLABS[h]:
        out.append(at)
        at += rows
    return out


def kernel(
    total_rows,
    part_ref,
    slot_ref,
    face_ref,
    near_ref,
    basis_hbm,
    jac_hbm,
    gal_ref,
    lspg_ref,
    out_hbm,
    basis,
    jac,
    send0, send1, send2, send3, send4, send5,
    one0, one1, one2, one3, one4, one5,
    two0, two1, two2, two3, two4, two5,
    tab0, tab1, tab2, tab3, tab4, tab5,
    face_out0, face_out1,
    halo0, halo1,
    meta,
    ints_v,
    ints_s,
    acc,
    core_in,
    pieces,
    plane_in,
    line_in,
    final,
    in_sem,
    out_sem,
    move_sem,
    local_sem,
):
    send = ((send0, send1, send2), (send3, send4, send5))
    one = ((one0, one1, one2), (one3, one4, one5))
    two = ((two0, two1, two2), (two3, two4, two5))
    tab = ((tab0, tab1, tab2), (tab3, tab4, tab5))
    face_out = (face_out0, face_out1)
    halo = (halo0, halo1)

    dom = lax.axis_index("dom")
    sub = lax.axis_index("sub")
    me = (dom // 4, dom % 4, sub // 2)
    core = sub % 2
    rank = dom * 8 + sub

    def device(shift, flip):
        x, y, z = [(a + b) % 4 for a, b in zip(me, shift)]
        return (x * 4 + y, z * 2 + (core + flip) % 2)

    def along(dim, step):
        shift = [0, 0, 0]
        shift[dim] = step
        return tuple(shift)

    def remote(src, dst, s_sem, r_sem, shift, flip):
        pltpu.make_async_remote_copy(
            src, dst, out_sem.at[s_sem], in_sem.at[r_sem],
            device_id=device(shift, flip), device_id_type=MESH,
        ).start()

    def local(src, dst, r_sem):
        pltpu.make_async_copy(src, dst, in_sem.at[r_sem]).start()

    def landed(view, r_sem):
        pltpu.make_async_copy(view, view, in_sem.at[r_sem]).wait()

    def sent(view, s_sem):
        pltpu.make_async_copy(view, view, out_sem.at[s_sem]).wait()

    basis_copy = pltpu.make_async_copy(basis_hbm, basis, move_sem.at[0])
    basis_copy.start()
    jac_copy = pltpu.make_async_copy(jac_hbm, jac, move_sem.at[1])
    jac_copy.start()

    peers = [((0, 0, 0), 1)]
    for dim in range(3):
        for step in (1, 2, 3):
            peers += [(along(dim, step), 0), (along(dim, step), 1)]
    for dx in (1, 2, 3):
        for dy in (1, 2, 3):
            peers.append(((dx, dy, 0), 0))
    barrier = pltpu.get_barrier_semaphore()
    for shift, flip in peers:
        pl.semaphore_signal(barrier, inc=1, device_id=device(shift, flip), device_id_type=MESH)

    lanes = lax.broadcasted_iota(I32, (1, 128), 1)

    def pick(b, carry):
        index, slot = carry
        hit = lanes == part_ref[b]
        return jnp.where(hit, b, index), jnp.where(hit, slot_ref[b], slot)

    index_row, slot_row = lax.fori_loop(
        0, 64, pick, (jnp.zeros((1, 128), I32), jnp.full((1, 128), -1, I32)), unroll=8
    )
    ints_v[0:1, :] = index_row
    mine = sub
    meta[me[0], me[1], mine] = slot_row
    ints_copy = pltpu.make_async_copy(ints_v, ints_s, local_sem.at[0])
    ints_copy.start()
    for h in range(2):
        for k in range(3):
            tab[h][k][128] = jnp.zeros(tab[h][k].shape[1:], BF16)
        halo[h][32] = jnp.zeros(halo[h].shape[1:], BF16)
    ints_copy.wait()
    basis_copy.wait()
    pl.semaphore_wait(barrier, len(peers))

    META_IN, META_OUT = 18, 18
    for step in (1, 2, 3):
        view = meta.at[me[0], me[1], mine]
        remote(view, view, META_OUT, META_IN, along(0, step), 0)

    def gather(h):
        base = offsets(h)

        def one_block(p, carry):
            block = basis[ints_s[0, p], :, h * 128:(h + 1) * 128]
            to = (p // 32, (p // 8) % 4, (p // 2) % 4)
            for k, (d1, d2, d3) in enumerate(ORDERS):
                rows = SLABS[h][k]
                send[h][k][to[d1] * 4 + to[d2], to[d3] * 2 + p % 2] = block[base[k]:base[k] + rows]
            return carry

        lax.fori_loop(0, 128, one_block, 0, unroll=4)

    def in_id(h, stage, k):
        return (h * 3 + stage) * 3 + k

    def stage1(h):
        for step in (1, 2, 3, 0):
            for k, (d1, d2, d3) in enumerate(ORDERS):
                to = (me[d1] + step) % 4
                src = send[h][k].at[pl.ds(to * 4, 4)]
                dst = one[h][k].at[me[d1]]
                if step:
                    remote(src, dst, in_id(h, 0, k), in_id(h, 0, k), along(d1, step), 0)
                else:
                    local(src, dst, in_id(h, 0, k))

    def stage2(h):
        for k, (d1, d2, d3) in enumerate(ORDERS):
            landed(one[h][k], in_id(h, 0, k))
            for step in (1, 2, 3, 0):
                to = (me[d2] + step) % 4
                src = one[h][k].at[:, to]
                dst = two[h][k].at[pl.ds(me[d2] * 4, 4)]
                if step:
                    remote(src, dst, in_id(h, 1, k), in_id(h, 1, k), along(d2, step), 0)
                else:
                    local(src, dst, in_id(h, 1, k))

    def stage3(h):
        for k, (d1, d2, d3) in enumerate(ORDERS):
            landed(two[h][k], in_id(h, 1, k))
            at = me[d3] * 2 + core
            dst = tab[h][k].at[pl.ds(at * 16, 16)]
            for step in (1, 2, 3, 0):
                for flip in (0, 1):
                    to = (me[d3] + step) % 4 * 2 + (core + flip) % 2
                    src = two[h][k].at[:, to]
                    if step or flip:
                        remote(src, dst, in_id(h, 2, k), in_id(h, 2, k), along(d3, step), flip)
                    else:
                        local(src, dst, in_id(h, 2, k))

    gather(0)
    stage1(0)
    gather(1)
    stage1(1)

    landed(meta.at[pl.ds(0, 3), 0, 0], META_IN)
    for step in (1, 2, 3):
        view = meta.at[:, me[1], mine]
        remote(view, view, META_OUT + 1, META_IN + 1, along(1, step), 0)
    stage2(0)
    stage2(1)
    landed(meta.at[pl.ds(0, 3), :, 0], META_IN + 1)
    for step in (0, 1, 2, 3):
        for flip in (0, 1):
            if step or flip:
                view = meta.at[:, :, mine]
                remote(view, view, META_OUT + 2, META_IN + 2, along(2, step), flip)
    stage3(0)
    stage3(1)

    landed(meta.at[:, :, pl.ds(0, 7)], META_IN + 2)
    arrived = meta[...].reshape(128, 1, 128)
    mine_only = lax.broadcasted_iota(I32, (128, 1, 128), 2) == rank
    slot_of = jnp.sum(jnp.where(mine_only, arrived, 0), axis=2, keepdims=True)
    hit = slot_of == lax.broadcasted_iota(I32, (128, 1, 128), 2)
    source = lax.broadcasted_iota(I32, (128, 1, 128), 0)
    from_ = (source // 32, (source // 8) % 4, (source // 2) % 4)
    for k, (d1, d2, d3) in enumerate(ORDERS):
        place = (from_[d3] * 2 + source % 2) * 16 + from_[d2] * 4 + from_[d1]
        ints_v[1 + k:2 + k, :] = jnp.max(jnp.where(hit, place, 0), axis=0)
    ints_v[4:5, :] = jnp.max(jnp.where(hit, 1, 0), axis=0)
    ints_copy = pltpu.make_async_copy(ints_v, ints_s, local_sem.at[0])
    ints_copy.start()
    ints_copy.wait()

    def table(h, slot):
        return jnp.concatenate([tab[h][k][ints_s[1 + k, slot]] for k in range(3)], axis=0)

    def entry(h, index):
        away = index >= 128
        slot = jnp.minimum(index, 127)
        slabs = [
            tab[h][k][jnp.where(away, 128, ints_s[1 + k, slot])] for k in range(3)
        ]
        near = jnp.concatenate(slabs, axis=0)
        return near + halo[h][jnp.where(away, index - 128, 32)]

    HALO_IN, HALO_OUT = 21, 21

    def send_faces(h):
        for k in range(3):
            landed(tab[h][k].at[pl.ds(0, 128)], in_id(h, 2, k))

        def one_face(e, carry):
            face_out[h][e] = table(h, face_ref[e])
            return carry

        lax.fori_loop(0, 4 * FACES, one_face, 0, unroll=2)
        dom_up = (((dom + 1) % 16), sub)
        dom_down = (((dom + 15) % 16), sub)
        sub_up = (dom, (sub + 1) % 8)
        sub_down = (dom, (sub + 7) % 8)
        moves = (
            (8, 8, 0, dom_up),
            (0, 8, 8, dom_down),
            (4, 4, 16, sub_up),
            (12, 4, 20, sub_up),
            (0, 4, 24, sub_down),
            (8, 4, 28, sub_down),
        )
        for src, count, dst, to in moves:
            pltpu.make_async_remote_copy(
                face_out[h].at[pl.ds(src, count)], halo[h].at[pl.ds(dst, count)],
                out_sem.at[HALO_OUT + h], in_sem.at[HALO_IN + h],
                device_id=to, device_id_type=MESH,
            ).start()

    def apply(h):
        landed(halo[h].at[pl.ds(0, 32)], HALO_IN + h)
        base = offsets(h)

        def one_slot(s, carry):
            own = table(h, s)
            first = entry(h, near_ref[s * 3 + 1])
            second = entry(h, near_ref[s * 3 + 2])
            right = jnp.concatenate([own, first, second], axis=0)
            left = jnp.concatenate([jac[s, 0], jac[s, 1], jac[s, 2]], axis=1)
            product = jnp.dot(left, right, preferred_element_type=F32)
            rows = (product * ints_s[4, s].astype(F32)).astype(BF16)
            for k in range(3):
                send[h][k][s // 8, s % 8] = rows[base[k]:base[k] + SLABS[h][k]]
            return carry

        lax.fori_loop(0, 128, one_slot, 0, unroll=4)
        for k in range(3):
            rows = SLABS[h][k]
            pltpu.make_async_copy(
                send[h][k],
                out_hbm.at[:, :, pl.ds(base[k], rows), pl.ds(h * 128, 128)],
                move_sem.at[2 + h * 3 + k],
            ).start()

    def stage1_sent(h):
        for k in range(3):
            sent(one[h][k].at[pl.ds(0, 3)], in_id(h, 0, k))

    send_faces(0)
    jac_copy.wait()
    stage1_sent(0)
    apply(0)
    send_faces(1)
    stage1_sent(1)
    apply(1)

    acc[...] = jnp.zeros_like(acc)

    def grams(g, carry):
        columns = []
        for h in range(2):
            columns.append(jnp.concatenate(
                [table(h, g * GL_SLOTS + e) for e in range(GL_SLOTS)], axis=0))
        for h in range(2):
            columns.append(jnp.concatenate(
                [send[h][k][(g * GL_SLOTS + e) // 8, (g * GL_SLOTS + e) % 8]
                 for e in range(GL_SLOTS) for k in range(3)], axis=0))
        basis_rows = jnp.concatenate(columns[:2], axis=1)
        rows = jnp.concatenate(columns[2:], axis=1)
        contract = (((0,), (0,)), ((), ()))
        acc[0] += lax.dot_general(basis_rows, rows, contract, preferred_element_type=F32)
        acc[1] += lax.dot_general(rows, rows, contract, preferred_element_type=F32)
        return carry

    lax.fori_loop(0, 128 // GL_SLOTS, grams, 0)

    SUM_IN, SUM_OUT = 23, 23
    other = ((0, 0, 0), 1)
    remote(acc.at[1 - core], core_in, SUM_OUT, SUM_IN, *other)
    landed(core_in, SUM_IN)
    pieces[...] = (acc[core] + core_in[...]).reshape(16, 16, 256)
    planes = [(dx, dy, 0) for dx in range(4) for dy in range(4) if dx or dy]
    for dx, dy, dz in planes:
        to = (me[0] + dx) % 4 * 4 + (me[1] + dy) % 4
        remote(pieces.at[to], plane_in.at[dom], SUM_OUT + 1, SUM_IN + 1, (dx, dy, 0), 0)
    plane_in[dom] = pieces[dom]
    landed(plane_in.at[pl.ds(0, 15)], SUM_IN + 1)
    line_in[me[2]] = jnp.sum(plane_in[...], axis=0)
    for step in (1, 2, 3):
        view = line_in.at[me[2]]
        remote(view, view, SUM_OUT + 2, SUM_IN + 2, along(2, step), 0)
    landed(line_in.at[pl.ds(0, 3)], SUM_IN + 2)
    final[core, dom] = jnp.sum(line_in[...], axis=0) * (1.0 / total_rows)
    for dx, dy, dz in planes:
        view = final.at[core, dom]
        remote(view, view, SUM_OUT + 3, SUM_IN + 3, (dx, dy, 0), 0)
    landed(final.at[0, pl.ds(0, 15)], SUM_IN + 3)
    remote(final.at[core], final.at[core], SUM_OUT + 4, SUM_IN + 4, *other)
    landed(final.at[0], SUM_IN + 4)
    gal_ref[...] = final[0].reshape(256, 256)
    lspg_ref[...] = final[1].reshape(256, 256)

    for h in range(2):
        for k in range(3):
            sent(two[h][k].at[pl.ds(0, 12)], in_id(h, 1, k))
            sent(tab[h][k].at[pl.ds(0, 112)], in_id(h, 2, k))
        sent(halo[h].at[pl.ds(0, 32)], HALO_OUT + h)
    sent(meta.at[pl.ds(0, 3), 0, 0], META_OUT)
    sent(meta.at[pl.ds(0, 3), :, 0], META_OUT + 1)
    sent(meta.at[:, :, pl.ds(0, 7)], META_OUT + 2)
    sent(core_in, SUM_OUT)
    sent(plane_in.at[pl.ds(0, 15)], SUM_OUT + 1)
    sent(line_in.at[pl.ds(0, 3)], SUM_OUT + 2)
    sent(final.at[0, pl.ds(0, 15)], SUM_OUT + 3)
    sent(final.at[0], SUM_OUT + 4)
    for h in range(2):
        base = offsets(h)
        for k in range(3):
            pltpu.make_async_copy(
                send[h][k],
                out_hbm.at[:, :, pl.ds(base[k], SLABS[h][k]), pl.ds(h * 128, 128)],
                move_sem.at[2 + h * 3 + k],
            ).wait()


def body(basis, block_part, block_slot, face_slots, neighbors, jacobian):
    total_rows = 128 * basis.shape[0]
    blocks = basis.reshape(64, 128, 256)
    slabs = [(h, k) for h in range(2) for k in range(3)]
    scratch = [pltpu.VMEM((64, 128, 256), BF16), pltpu.VMEM((128, 3, 128, 128), BF16)]
    scratch += [pltpu.VMEM((16, 8, SLABS[h][k], 128), BF16) for h, k in slabs]
    scratch += [pltpu.VMEM((4, 4, 8, SLABS[h][k], 128), BF16) for h, k in slabs]
    scratch += [pltpu.VMEM((16, 8, SLABS[h][k], 128), BF16) for h, k in slabs]
    scratch += [pltpu.VMEM((129, SLABS[h][k], 128), BF16) for h, k in slabs]
    scratch += [pltpu.VMEM((16, 128, 128), BF16)] * 2
    scratch += [pltpu.VMEM((33, 128, 128), BF16)] * 2
    scratch += [
        pltpu.VMEM((4, 4, 8, 1, 128), I32),
        pltpu.VMEM((8, 128), I32),
        pltpu.SMEM((8, 128), I32),
        pltpu.VMEM((2, 256, 256), F32),
        pltpu.VMEM((256, 256), F32),
        pltpu.VMEM((16, 16, 256), F32),
        pltpu.VMEM((16, 16, 256), F32),
        pltpu.VMEM((4, 16, 256), F32),
        pltpu.VMEM((2, 16, 16, 256), F32),
        pltpu.SemaphoreType.DMA((28,)),
        pltpu.SemaphoreType.DMA((28,)),
        pltpu.SemaphoreType.DMA((8,)),
        pltpu.SemaphoreType.DMA((1,)),
    ]
    smem = pl.BlockSpec(memory_space=pltpu.SMEM)
    vmem = pl.BlockSpec(memory_space=pltpu.VMEM)
    anywhere = pl.BlockSpec(memory_space=pl.ANY)
    galerkin, lspg, applied = pl.pallas_call(
        functools.partial(kernel, total_rows),
        out_shape=(
            jax.ShapeDtypeStruct((256, 256), F32),
            jax.ShapeDtypeStruct((256, 256), F32),
            jax.ShapeDtypeStruct((16, 8, 128, 256), BF16),
        ),
        in_specs=[smem, smem, smem, smem, anywhere, anywhere],
        out_specs=(vmem, vmem, anywhere),
        scratch_shapes=scratch,
        compiler_params=pltpu.CompilerParams(
            collective_id=0, has_side_effects=True, vmem_limit_bytes=60 * 2**20
        ),
        cost_estimate=pl.CostEstimate(
            flops=7_500_000_000, bytes_accessed=25_000_000, transcendentals=0
        ),
        name="regroup_apply_reduce",
    )(block_part, block_slot, face_slots.reshape(-1), neighbors.reshape(-1), blocks, jacobian)
    return galerkin, lspg, applied.reshape(16384, 256)


def solution(mesh):
    in_specs = (
        P(("dom", "sub"), None),
        P(("dom", "sub")),
        P(("dom", "sub")),
        P(("dom", "sub"), None),
        P(("dom", "sub"), None),
        P(("dom", "sub"), None, None, None),
    )
    out_specs = (P(), P(), P(("dom", "sub"), None))
    return jax.shard_map(body, mesh=mesh, in_specs=in_specs, out_specs=out_specs, check_vma=False)
```

```python
import functools

import jax
import jax.numpy as jnp
from jax import lax
from jax.experimental import pallas as pl
from jax.experimental.pallas import tpu as pltpu
from jax.sharding import PartitionSpec as P

MESH = pl.DeviceIdType.MESH
BF16 = jnp.bfloat16
F32 = jnp.float32
I32 = jnp.int32

SLABS = ((48, 32, 48), (48, 48, 32))
ORDERS = ((0, 1, 2), (1, 2, 0), (2, 0, 1))
FACES = 4
BATCH = 16
BEFORE = 3
EARLY = ((1, 0), (3, 0), (1, 1), (3, 1))
LATE = ((2, 0), (2, 1), (0, 1), (0, 0))


def offsets(h):
    out, at = [], 0
    for rows in SLABS[h]:
        out.append(at)
        at += rows
    return out


def kernel(
    total_rows,
    part_ref,
    slot_ref,
    face_ref,
    near_ref,
    basis_hbm,
    jac_hbm,
    gal_ref,
    lspg_ref,
    out_ref,
    basis,
    jac,
    one0, one1, one2, one3, one4, one5,
    two0, two1, two2, two3, two4, two5,
    tab0, tab1, tab2, tab3, tab4, tab5,
    face_out0, face_out1,
    halo0, halo1,
    meta,
    ints_v,
    ints_s,
    acc,
    core_in,
    pieces,
    plane_in,
    line_in,
    final,
    in_sem,
    out_sem,
    move_sem,
    local_sem,
):
    one = ((one0, one1, one2), (one3, one4, one5))
    two = ((two0, two1, two2), (two3, two4, two5))
    tab = ((tab0, tab1, tab2), (tab3, tab4, tab5))
    face_out = (face_out0, face_out1)
    halo = (halo0, halo1)

    dom = lax.axis_index("dom")
    sub = lax.axis_index("sub")
    me = (dom // 4, dom % 4, sub // 2)
    core = sub % 2
    rank = dom * 8 + sub

    def device(shift, flip):
        x, y, z = [(a + b) % 4 for a, b in zip(me, shift)]
        return (x * 4 + y, z * 2 + (core + flip) % 2)

    def along(dim, step):
        shift = [0, 0, 0]
        shift[dim] = step
        return tuple(shift)

    def remote(src, dst, s_sem, r_sem, shift, flip):
        pltpu.make_async_remote_copy(
            src, dst, out_sem.at[s_sem], in_sem.at[r_sem],
            device_id=device(shift, flip), device_id_type=MESH,
        ).start()

    def local(src, dst, r_sem):
        pltpu.make_async_copy(src, dst, in_sem.at[r_sem]).start()

    def landed(view, r_sem):
        pltpu.make_async_copy(view, view, in_sem.at[r_sem]).wait()

    def sent(view, s_sem):
        pltpu.make_async_copy(view, view, out_sem.at[s_sem]).wait()

    basis_copy = pltpu.make_async_copy(basis_hbm, basis, move_sem.at[0])
    basis_copy.start()
    jac_copy = pltpu.make_async_copy(jac_hbm, jac, move_sem.at[1])
    jac_copy.start()

    peers = [((0, 0, 0), 1)]
    for dim in range(3):
        for step in (1, 2, 3):
            peers += [(along(dim, step), 0), (along(dim, step), 1)]
    for dx in (1, 2, 3):
        for dy in (1, 2, 3):
            peers.append(((dx, dy, 0), 0))
    barrier = pltpu.get_barrier_semaphore()
    for shift, flip in peers:
        pl.semaphore_signal(barrier, inc=1, device_id=device(shift, flip), device_id_type=MESH)

    lanes = lax.broadcasted_iota(I32, (1, 128), 1)

    def pick(b, carry):
        index, slot = carry
        hit = lanes == part_ref[b]
        return jnp.where(hit, b, index), jnp.where(hit, slot_ref[b], slot)

    index_row, slot_row = lax.fori_loop(
        0, 64, pick, (jnp.zeros((1, 128), I32), jnp.full((1, 128), -1, I32)), unroll=8
    )
    ints_v[0:1, :] = index_row
    mine = sub
    meta[me[0], me[1], mine] = slot_row
    ints_copy = pltpu.make_async_copy(ints_v, ints_s, local_sem.at[0])
    ints_copy.start()
    for h in range(2):
        for k in range(3):
            tab[h][k][128] = jnp.zeros(tab[h][k].shape[1:], BF16)
        halo[h][32] = jnp.zeros(halo[h].shape[1:], BF16)
    ints_copy.wait()
    basis_copy.wait()
    pl.semaphore_wait(barrier, len(peers))

    META_IN, META_OUT = 18, 18
    for step in (1, 2, 3):
        view = meta.at[me[0], me[1], mine]
        remote(view, view, META_OUT, META_IN, along(0, step), 0)

    def gather(h):
        base = offsets(h)

        def one_block(p, carry):
            block = basis[ints_s[0, p], :, h * 128:(h + 1) * 128]
            to = (p // 32, (p // 8) % 4, (p // 2) % 4)
            for k, (d1, d2, d3) in enumerate(ORDERS):
                rows = SLABS[h][k]
                out_ref[to[d1] * 4 + to[d2], to[d3] * 2 + p % 2, base[k]:base[k] + rows,
                        h * 128:(h + 1) * 128] = block[base[k]:base[k] + rows]
            return carry

        lax.fori_loop(0, 128, one_block, 0, unroll=4)

    def in_id(h, stage, k):
        return (h * 3 + stage) * 3 + k

    def stage1(h, k):
        d1, d2, d3 = ORDERS[k]
        for step in (1, 2, 3, 0):
            to = (me[d1] + step) % 4
            src = out_ref.at[
                pl.ds(to * 4, 4), :, pl.ds(offsets(h)[k], SLABS[h][k]), pl.ds(h * 128, 128)]
            dst = one[h][k].at[me[d1]]
            if step:
                remote(src, dst, in_id(h, 0, k), in_id(h, 0, k), along(d1, step), 0)
            else:
                local(src, dst, in_id(h, 0, k))

    def stage2(h, k):
        d1, d2, d3 = ORDERS[k]
        for step in (1, 2, 3, 0):
            to = (me[d2] + step) % 4
            src = one[h][k].at[:, to]
            dst = two[h][k].at[pl.ds(me[d2] * 4, 4)]
            if step:
                remote(src, dst, in_id(h, 1, k), in_id(h, 1, k), along(d2, step), 0)
            else:
                local(src, dst, in_id(h, 1, k))

    def stage3(h, k, moves):
        d1, d2, d3 = ORDERS[k]
        dst = tab[h][k].at[pl.ds((me[d3] * 2 + core) * 16, 16)]
        for step, flip in moves:
            to = (me[d3] + step) % 4 * 2 + (core + flip) % 2
            src = two[h][k].at[:, to]
            if step or flip:
                remote(src, dst, in_id(h, 2, k), in_id(h, 2, k), along(d3, step), flip)
            else:
                local(src, dst, in_id(h, 2, k))

    gather(0)
    for k in range(3):
        stage1(0, k)
    gather(1)
    for k in range(3):
        stage1(1, k)
    for h in range(2):
        for k in range(3):
            landed(one[h][k], in_id(h, 0, k))
            stage2(h, k)
    landed(meta.at[pl.ds(0, 3), 0, 0], META_IN)
    for step in (1, 2, 3):
        view = meta.at[:, me[1], mine]
        remote(view, view, META_OUT + 1, META_IN + 1, along(1, step), 0)
    for k in range(3):
        landed(two[0][k], in_id(0, 1, k))
        stage3(0, k, EARLY + LATE)
    landed(meta.at[pl.ds(0, 3), :, 0], META_IN + 1)
    for step in (0, 1, 2, 3):
        for flip in (0, 1):
            if step or flip:
                view = meta.at[:, :, mine]
                remote(view, view, META_OUT + 2, META_IN + 2, along(2, step), flip)
    for k in range(3):
        landed(two[1][k], in_id(1, 1, k))
        stage3(1, k, EARLY)

    landed(meta.at[:, :, pl.ds(0, 7)], META_IN + 2)
    arrived = meta[...].reshape(128, 1, 128)
    mine_only = lax.broadcasted_iota(I32, (128, 1, 128), 2) == rank
    slot_of = jnp.sum(jnp.where(mine_only, arrived, 0), axis=2, keepdims=True)
    hit = slot_of == lax.broadcasted_iota(I32, (128, 1, 128), 2)
    source = lax.broadcasted_iota(I32, (128, 1, 128), 0)
    from_ = (source // 32, (source // 8) % 4, (source // 2) % 4)
    for k, (d1, d2, d3) in enumerate(ORDERS):
        place = (from_[d3] * 2 + source % 2) * 16 + from_[d2] * 4 + from_[d1]
        ints_v[1 + k:2 + k, :] = jnp.max(jnp.where(hit, place, 0), axis=0)
    ints_v[4:5, :] = jnp.max(jnp.where(hit, 1, 0), axis=0)
    ints_copy = pltpu.make_async_copy(ints_v, ints_s, local_sem.at[0])
    ints_copy.start()
    ints_copy.wait()

    def table(h, slot):
        return jnp.concatenate([tab[h][k][ints_s[1 + k, slot]] for k in range(3)], axis=0)

    def entry(h, index):
        away = index >= 128
        slot = jnp.minimum(index, 127)
        slabs = [
            tab[h][k][jnp.where(away, 128, ints_s[1 + k, slot])] for k in range(3)
        ]
        near = jnp.concatenate(slabs, axis=0)
        return near + halo[h][jnp.where(away, index - 128, 32)]

    HALO_IN, HALO_OUT = 21, 21

    def send_faces(h):
        for k in range(3):
            landed(tab[h][k].at[pl.ds(0, 128)], in_id(h, 2, k))

        def one_face(e, carry):
            face_out[h][e] = table(h, face_ref[e // FACES, e % FACES])
            return carry

        lax.fori_loop(0, 4 * FACES, one_face, 0, unroll=2)
        dom_up = (((dom + 1) % 16), sub)
        dom_down = (((dom + 15) % 16), sub)
        sub_up = (dom, (sub + 1) % 8)
        sub_down = (dom, (sub + 7) % 8)
        moves = (
            (8, 8, 0, dom_up),
            (0, 8, 8, dom_down),
            (4, 4, 16, sub_up),
            (12, 4, 20, sub_up),
            (0, 4, 24, sub_down),
            (8, 4, 28, sub_down),
        )
        for src, count, dst, to in moves:
            pltpu.make_async_remote_copy(
                face_out[h].at[pl.ds(src, count)], halo[h].at[pl.ds(dst, count)],
                out_sem.at[HALO_OUT + h], in_sem.at[HALO_IN + h],
                device_id=to, device_id_type=MESH,
            ).start()

    contract = (((0,), (0,)), ((), ()))

    def tables(h, first):
        return jnp.concatenate([table(h, first + e) for e in range(BATCH)], axis=0)

    def applied(h, g):
        per = BATCH // 8
        rows = out_ref[pl.ds(g * per, per), :, :, h * 128:(h + 1) * 128]
        return rows.reshape(BATCH * 128, 128)

    def apply(h, low, high):
        def some_slots(g, carry):
            done = []
            for e in range(BATCH):
                s = g * BATCH + e
                right = jnp.concatenate(
                    [table(h, s), entry(h, near_ref[1, s]), entry(h, near_ref[2, s])], axis=0)
                left = jnp.concatenate([jac[s, 0], jac[s, 1], jac[s, 2]], axis=1)
                product = jnp.dot(left, right, preferred_element_type=F32)
                rows = (product * ints_s[4, s].astype(F32)).astype(BF16)
                out_ref[s // 8, s % 8, :, h * 128:(h + 1) * 128] = rows
                done.append(rows)
            rows = jnp.concatenate(done, axis=0)
            first = g * BATCH
            if h == 0:
                right = jnp.concatenate([tables(0, first), rows], axis=1)
                gram = lax.dot_general(rows, right, contract, preferred_element_type=F32)
                acc[0, :128, :128] += gram[:, :128]
                acc[1, :128, :128] += gram[:, 128:]
            else:
                right = jnp.concatenate(
                    [tables(0, first), tables(1, first), applied(0, g), rows], axis=1)
                gram = lax.dot_general(rows, right, contract, preferred_element_type=F32)
                acc[0, 128:, :] += gram[:, :256]
                acc[1, 128:, :] += gram[:, 256:]
            return carry

        lax.fori_loop(low, high, some_slots, 0)

    def gram_across():
        def some_slots(g, carry):
            acc[0, :128, 128:] += lax.dot_general(
                applied(0, g), tables(1, g * BATCH), contract, preferred_element_type=F32)
            return carry

        lax.fori_loop(0, 128 // BATCH, some_slots, 0)

    acc[...] = jnp.zeros_like(acc)
    send_faces(0)
    for k in range(3):
        stage3(1, k, LATE)
    for h in range(2):
        for k in range(3):
            sent(one[h][k].at[pl.ds(0, 3)], in_id(h, 0, k))
    jac_copy.wait()
    landed(halo[0].at[pl.ds(0, 32)], HALO_IN)
    apply(0, 0, BEFORE)
    send_faces(1)
    apply(0, BEFORE, 128 // BATCH)
    gram_across()
    landed(halo[1].at[pl.ds(0, 32)], HALO_IN + 1)
    apply(1, 0, 128 // BATCH)

    SUM_IN, SUM_OUT = 23, 23
    other = ((0, 0, 0), 1)
    remote(acc.at[1 - core], core_in, SUM_OUT, SUM_IN, *other)
    landed(core_in, SUM_IN)
    pieces[...] = (acc[core] + core_in[...]).reshape(16, 16, 256)
    planes = [(dx, dy, 0) for dx in range(4) for dy in range(4) if dx or dy]
    for dx, dy, dz in planes:
        to = (me[0] + dx) % 4 * 4 + (me[1] + dy) % 4
        remote(pieces.at[to], plane_in.at[dom], SUM_OUT + 1, SUM_IN + 1, (dx, dy, 0), 0)
    plane_in[dom] = pieces[dom]
    landed(plane_in.at[pl.ds(0, 15)], SUM_IN + 1)
    line_in[me[2]] = jnp.sum(plane_in[...], axis=0)
    for step in (1, 2, 3):
        view = line_in.at[me[2]]
        remote(view, view, SUM_OUT + 2, SUM_IN + 2, along(2, step), 0)
    landed(line_in.at[pl.ds(0, 3)], SUM_IN + 2)
    final[core, dom] = jnp.sum(line_in[...], axis=0) * (1.0 / total_rows)
    view = final.at[core, dom]
    for n, (dx, dy, dz) in enumerate(planes):
        remote(view, view, SUM_OUT + 3, SUM_IN + 4 + n, (dx, dy, 0), 0)
    remote(view, view, SUM_OUT + 4, SUM_IN + 3, *other)
    for n, (dx, dy, dz) in enumerate(planes):
        view = final.at[core, (me[0] - dx) % 4 * 4 + (me[1] - dy) % 4]
        landed(view, SUM_IN + 4 + n)
        remote(view, view, SUM_OUT + 4, SUM_IN + 3, *other)
    landed(final.at[0], SUM_IN + 3)
    flipped = final[0].reshape(256, 256)
    lower = final[1].reshape(256, 256)
    gal_ref[...] = flipped.T
    lspg_ref[...] = lower
    lspg_ref[:128, 128:] = lower[128:, :128].T

    for h in range(2):
        for k in range(3):
            sent(two[h][k].at[pl.ds(0, 12)], in_id(h, 1, k))
            sent(tab[h][k].at[pl.ds(0, 112)], in_id(h, 2, k))
        sent(halo[h].at[pl.ds(0, 32)], HALO_OUT + h)
    sent(meta.at[pl.ds(0, 3), 0, 0], META_OUT)
    sent(meta.at[pl.ds(0, 3), :, 0], META_OUT + 1)
    sent(meta.at[:, :, pl.ds(0, 7)], META_OUT + 2)
    sent(core_in, SUM_OUT)
    sent(plane_in.at[pl.ds(0, 15)], SUM_OUT + 1)
    sent(line_in.at[pl.ds(0, 3)], SUM_OUT + 2)
    sent(final.at[0, pl.ds(0, 15)], SUM_OUT + 3)
    sent(final.at[0], SUM_OUT + 4)


def body(basis, block_part, block_slot, face_slots, neighbors, jacobian):
    total_rows = 128 * basis.shape[0]
    blocks = basis.reshape(64, 128, 256)
    slabs = [(h, k) for h in range(2) for k in range(3)]
    scratch = [pltpu.VMEM((64, 128, 256), BF16), pltpu.VMEM((128, 3, 128, 128), BF16)]
    scratch += [pltpu.VMEM((4, 4, 8, SLABS[h][k], 128), BF16) for h, k in slabs]
    scratch += [pltpu.VMEM((16, 8, SLABS[h][k], 128), BF16) for h, k in slabs]
    scratch += [pltpu.VMEM((129, SLABS[h][k], 128), BF16) for h, k in slabs]
    scratch += [pltpu.VMEM((16, 128, 128), BF16)] * 2
    scratch += [pltpu.VMEM((33, 128, 128), BF16)] * 2
    scratch += [
        pltpu.VMEM((4, 4, 8, 1, 128), I32),
        pltpu.VMEM((8, 128), I32),
        pltpu.SMEM((8, 128), I32),
        pltpu.VMEM((2, 256, 256), F32),
        pltpu.VMEM((256, 256), F32),
        pltpu.VMEM((16, 16, 256), F32),
        pltpu.VMEM((16, 16, 256), F32),
        pltpu.VMEM((4, 16, 256), F32),
        pltpu.VMEM((2, 16, 16, 256), F32),
        pltpu.SemaphoreType.DMA((42,)),
        pltpu.SemaphoreType.DMA((28,)),
        pltpu.SemaphoreType.DMA((2,)),
        pltpu.SemaphoreType.DMA((1,)),
    ]
    smem = pl.BlockSpec(memory_space=pltpu.SMEM)
    vmem = pl.BlockSpec(memory_space=pltpu.VMEM)
    anywhere = pl.BlockSpec(memory_space=pl.ANY)
    galerkin, lspg, applied = pl.pallas_call(
        functools.partial(kernel, total_rows),
        out_shape=(
            pltpu.VMEM((256, 256), F32),
            pltpu.VMEM((256, 256), F32),
            pltpu.VMEM((16, 8, 128, 256), BF16),
        ),
        in_specs=[smem, smem, smem, smem, anywhere, anywhere],
        out_specs=(vmem, vmem, vmem),
        scratch_shapes=scratch,
        compiler_params=pltpu.CompilerParams(
            collective_id=0, has_side_effects=True, vmem_limit_bytes=54 * 2**20
        ),
        cost_estimate=pl.CostEstimate(
            flops=7_500_000_000, bytes_accessed=25_000_000, transcendentals=0
        ),
        name="regroup_apply_reduce",
    )(block_part, block_slot, face_slots, neighbors.T, blocks, jacobian)
    return galerkin, lspg, applied.reshape(16384, 256)


def solution(mesh):
    in_specs = (
        P(("dom", "sub"), None),
        P(("dom", "sub")),
        P(("dom", "sub")),
        P(("dom", "sub"), None),
        P(("dom", "sub"), None),
        P(("dom", "sub"), None, None, None),
    )
    out_specs = (P(), P(), P(("dom", "sub"), None))
    return jax.shard_map(body, mesh=mesh, in_specs=in_specs, out_specs=out_specs, check_vma=False)
```

```python
import functools

import jax
import jax.numpy as jnp
from jax import lax
from jax.experimental import pallas as pl
from jax.experimental.pallas import tpu as pltpu
from jax.sharding import PartitionSpec as P

MESH = pl.DeviceIdType.MESH
BF16 = jnp.bfloat16
F32 = jnp.float32
I32 = jnp.int32

SLABS = ((48, 32, 48), (48, 48, 32))
ORDERS = ((0, 1, 2), (1, 2, 0), (2, 0, 1))
FACES = 4
PARTS = 4
BATCH = 32
BEFORE = 3
EARLY = ((1, 0), (3, 0), (1, 1), (3, 1))
LATE = ((2, 0), (2, 1), (0, 1), (0, 0))


def offsets(h):
    out, at = [], 0
    for rows in SLABS[h]:
        out.append(at)
        at += rows
    return out


def kernel(
    total_rows,
    part_ref,
    slot_ref,
    face_ref,
    near_ref,
    basis_hbm,
    jac_hbm,
    gal_ref,
    lspg_ref,
    out_ref,
    basis,
    jac,
    one0, one1, one2, one3, one4, one5,
    two0, two1, two2, two3, two4, two5,
    tab0, tab1, tab2, tab3, tab4, tab5,
    face_out0, face_out1,
    halo0, halo1,
    meta,
    ints_v,
    ints_s,
    acc,
    core_in,
    pieces,
    plane_in,
    line_in,
    final,
    in_sem,
    out_sem,
    move_sem,
    local_sem,
):
    one = ((one0, one1, one2), (one3, one4, one5))
    two = ((two0, two1, two2), (two3, two4, two5))
    tab = ((tab0, tab1, tab2), (tab3, tab4, tab5))
    face_out = (face_out0, face_out1)
    halo = (halo0, halo1)

    dom = lax.axis_index("dom")
    sub = lax.axis_index("sub")
    me = (dom // 4, dom % 4, sub // 2)
    core = sub % 2
    rank = dom * 8 + sub

    def device(shift, flip):
        x, y, z = [(a + b) % 4 for a, b in zip(me, shift)]
        return (x * 4 + y, z * 2 + (core + flip) % 2)

    def along(dim, step):
        shift = [0, 0, 0]
        shift[dim] = step
        return tuple(shift)

    def remote(src, dst, s_sem, r_sem, shift, flip):
        pltpu.make_async_remote_copy(
            src, dst, out_sem.at[s_sem], in_sem.at[r_sem],
            device_id=device(shift, flip), device_id_type=MESH,
        ).start()

    def local(src, dst, r_sem):
        pltpu.make_async_copy(src, dst, in_sem.at[r_sem]).start()

    def landed(view, r_sem):
        pltpu.make_async_copy(view, view, in_sem.at[r_sem]).wait()

    def sent(view, s_sem):
        pltpu.make_async_copy(view, view, out_sem.at[s_sem]).wait()

    basis_copy = pltpu.make_async_copy(basis_hbm, basis, move_sem.at[0])
    basis_copy.start()
    jac_copy = pltpu.make_async_copy(jac_hbm, jac, move_sem.at[1])

    peers = [((0, 0, 0), 1)]
    for dim in range(3):
        for step in (1, 2, 3):
            peers += [(along(dim, step), 0), (along(dim, step), 1)]
    for dx in (1, 2, 3):
        for dy in (1, 2, 3):
            peers.append(((dx, dy, 0), 0))
    barrier = pltpu.get_barrier_semaphore()
    for shift, flip in peers:
        pl.semaphore_signal(barrier, inc=1, device_id=device(shift, flip), device_id_type=MESH)

    lanes = lax.broadcasted_iota(I32, (1, 128), 1)

    def pick(b, carry):
        index, slot = carry
        hit = lanes == part_ref[b]
        return jnp.where(hit, b, index), jnp.where(hit, slot_ref[b], slot)

    index_row, slot_row = lax.fori_loop(
        0, 64, pick, (jnp.zeros((1, 128), I32), jnp.full((1, 128), -1, I32)), unroll=8
    )
    ints_v[0:1, :] = index_row
    mine = sub
    meta[me[0], me[1], mine] = slot_row
    ints_copy = pltpu.make_async_copy(ints_v, ints_s, local_sem.at[0])
    ints_copy.start()
    for h in range(2):
        for k in range(3):
            tab[h][k][128] = jnp.zeros(tab[h][k].shape[1:], BF16)
        halo[h][32] = jnp.zeros(halo[h].shape[1:], BF16)
    ints_copy.wait()
    basis_copy.wait()
    jac_copy.start()

    def gather(h):
        base = offsets(h)

        def one_block(p, carry):
            block = basis[ints_s[0, p], :, h * 128:(h + 1) * 128]
            to = (p // 32, (p // 8) % 4, (p // 2) % 4)
            for k, (d1, d2, d3) in enumerate(ORDERS):
                rows = SLABS[h][k]
                out_ref[to[d1] * 4 + to[d2], to[d3] * 2 + p % 2, base[k]:base[k] + rows,
                        h * 128:(h + 1) * 128] = block[base[k]:base[k] + rows]
            return carry

        lax.fori_loop(0, 128, one_block, 0, unroll=4)

    def in_id(h, stage, k):
        return (h * 3 + stage) * 3 + k

    def stage1(h, k):
        d1, d2, d3 = ORDERS[k]
        for step in (1, 2, 3, 0):
            to = (me[d1] + step) % 4
            src = out_ref.at[
                pl.ds(to * 4, 4), :, pl.ds(offsets(h)[k], SLABS[h][k]), pl.ds(h * 128, 128)]
            dst = one[h][k].at[me[d1]]
            if step:
                remote(src, dst, in_id(h, 0, k), in_id(h, 0, k), along(d1, step), 0)
            else:
                local(src, dst, in_id(h, 0, k))

    def stage2(h, k):
        d1, d2, d3 = ORDERS[k]
        for step in (1, 2, 3, 0):
            to = (me[d2] + step) % 4
            src = one[h][k].at[:, to]
            dst = two[h][k].at[pl.ds(me[d2] * 4, 4)]
            if step:
                remote(src, dst, in_id(h, 1, k), in_id(h, 1, k), along(d2, step), 0)
            else:
                local(src, dst, in_id(h, 1, k))

    def stage3(h, k, moves):
        d1, d2, d3 = ORDERS[k]
        dst = tab[h][k].at[pl.ds((me[d3] * 2 + core) * 16, 16)]
        for step, flip in moves:
            to = (me[d3] + step) % 4 * 2 + (core + flip) % 2
            src = two[h][k].at[:, to]
            if step or flip:
                remote(src, dst, in_id(h, 2, k), in_id(h, 2, k), along(d3, step), flip)
            else:
                local(src, dst, in_id(h, 2, k))

    gather(0)
    pl.semaphore_wait(barrier, len(peers))

    META_IN, META_OUT = 18, 18
    for step in (1, 2, 3):
        view = meta.at[me[0], me[1], mine]
        remote(view, view, META_OUT, META_IN, along(0, step), 0)

    for k in (1, 0, 2):
        stage1(0, k)
    gather(1)
    for k in (1, 0, 2):
        stage1(1, k)
    for h in range(2):
        for k in range(3):
            landed(one[h][k], in_id(h, 0, k))
            stage2(h, k)
    landed(meta.at[pl.ds(0, 3), 0, 0], META_IN)
    for step in (1, 2, 3):
        view = meta.at[:, me[1], mine]
        remote(view, view, META_OUT + 1, META_IN + 1, along(1, step), 0)
    for k in (2, 0, 1):
        landed(two[0][k], in_id(0, 1, k))
        stage3(0, k, EARLY + LATE)
    landed(meta.at[pl.ds(0, 3), :, 0], META_IN + 1)
    for step in (0, 1, 2, 3):
        for flip in (0, 1):
            if step or flip:
                view = meta.at[:, :, mine]
                remote(view, view, META_OUT + 2, META_IN + 2, along(2, step), flip)
    for k in (2, 0, 1):
        landed(two[1][k], in_id(1, 1, k))
        stage3(1, k, EARLY)

    landed(meta.at[:, :, pl.ds(0, 7)], META_IN + 2)
    arrived = meta[...].reshape(128, 1, 128)
    mine_only = lax.broadcasted_iota(I32, (128, 1, 128), 2) == rank
    slot_of = jnp.sum(jnp.where(mine_only, arrived, 0), axis=2, keepdims=True)
    hit = slot_of == lax.broadcasted_iota(I32, (128, 1, 128), 2)
    source = lax.broadcasted_iota(I32, (128, 1, 128), 0)
    from_ = (source // 32, (source // 8) % 4, (source // 2) % 4)
    for k, (d1, d2, d3) in enumerate(ORDERS):
        place = (from_[d3] * 2 + source % 2) * 16 + from_[d2] * 4 + from_[d1]
        ints_v[1 + k:2 + k, :] = jnp.max(jnp.where(hit, place, 0), axis=0)
    ints_v[4:5, :] = jnp.max(jnp.where(hit, 1, 0), axis=0)
    ints_copy = pltpu.make_async_copy(ints_v, ints_s, local_sem.at[0])
    ints_copy.start()
    ints_copy.wait()

    def table(h, slot):
        return jnp.concatenate([tab[h][k][ints_s[1 + k, slot]] for k in range(3)], axis=0)

    def entry(h, index):
        away = index >= 128
        slot = jnp.minimum(index, 127)
        slabs = [
            tab[h][k][jnp.where(away, 128, ints_s[1 + k, slot])] for k in range(3)
        ]
        near = jnp.concatenate(slabs, axis=0)
        return near + halo[h][jnp.where(away, index - 128, 32)]

    HALO_IN, HALO_OUT = 21, 21

    def send_faces(h):
        for k in range(3):
            landed(tab[h][k].at[pl.ds(0, 128)], in_id(h, 2, k))

        def one_face(e, carry):
            face_out[h][e] = table(h, face_ref[e // FACES, e % FACES])
            return carry

        lax.fori_loop(0, 4 * FACES, one_face, 0, unroll=2)
        dom_up = (((dom + 1) % 16), sub)
        dom_down = (((dom + 15) % 16), sub)
        sub_up = (dom, (sub + 1) % 8)
        sub_down = (dom, (sub + 7) % 8)
        moves = (
            (8, 8, 0, dom_up),
            (0, 8, 8, dom_down),
            (4, 4, 16, sub_up),
            (12, 4, 20, sub_up),
            (0, 4, 24, sub_down),
            (8, 4, 28, sub_down),
        )
        for src, count, dst, to in moves:
            pltpu.make_async_remote_copy(
                face_out[h].at[pl.ds(src, count)], halo[h].at[pl.ds(dst, count)],
                out_sem.at[HALO_OUT + h], in_sem.at[HALO_IN + h],
                device_id=to, device_id_type=MESH,
            ).start()

    contract = (((0,), (0,)), ((), ()))

    def tables(h, first):
        return jnp.concatenate([table(h, first + e) for e in range(BATCH)], axis=0)

    def applied(h, g):
        per = BATCH // 8
        rows = out_ref[pl.ds(g * per, per), :, :, h * 128:(h + 1) * 128]
        return rows.reshape(BATCH * 128, 128)

    def apply(h, low, high):
        def some_slots(g, carry):
            done = []
            for e in range(BATCH):
                s = g * BATCH + e
                right = jnp.concatenate(
                    [table(h, s), entry(h, near_ref[1, s]), entry(h, near_ref[2, s])], axis=0)
                left = jnp.concatenate([jac[s, 0], jac[s, 1], jac[s, 2]], axis=1)
                product = jnp.dot(left, right, preferred_element_type=F32)
                rows = (product * ints_s[4, s].astype(F32)).astype(BF16)
                out_ref[s // 8, s % 8, :, h * 128:(h + 1) * 128] = rows
                done.append(rows)
            rows = jnp.concatenate(done, axis=0)
            first = g * BATCH
            if h == 0:
                right = jnp.concatenate([tables(0, first), rows], axis=1)
                gram = lax.dot_general(rows, right, contract, preferred_element_type=F32)
                acc[0, :128, :128] += gram[:, :128]
                acc[1, :128, :128] += gram[:, 128:]
            else:
                right = jnp.concatenate(
                    [tables(0, first), tables(1, first), applied(0, g), rows], axis=1)
                gram = lax.dot_general(rows, right, contract, preferred_element_type=F32)
                acc[0, 128:, :] += gram[:, :256]
                acc[1, 128:, :] += gram[:, 256:]
            return carry

        lax.fori_loop(low, high, some_slots, 0)

    def gram_across():
        def some_slots(g, carry):
            acc[0, :128, 128:] += lax.dot_general(
                applied(0, g), tables(1, g * BATCH), contract, preferred_element_type=F32)
            return carry

        lax.fori_loop(0, 128 // BATCH, some_slots, 0)

    acc[...] = jnp.zeros_like(acc)
    send_faces(0)
    for k in (2, 0, 1):
        stage3(1, k, LATE)
    for h in range(2):
        for k in range(3):
            sent(one[h][k].at[pl.ds(0, 3)], in_id(h, 0, k))
    jac_copy.wait()
    landed(halo[0].at[pl.ds(0, 32)], HALO_IN)
    apply(0, 0, BEFORE)
    send_faces(1)
    apply(0, BEFORE, 128 // BATCH)
    gram_across()
    landed(halo[1].at[pl.ds(0, 32)], HALO_IN + 1)
    apply(1, 0, 128 // BATCH)

    SUM_IN, SUM_OUT = 23, 23
    other = ((0, 0, 0), 1)
    remote(acc.at[1 - core], core_in, SUM_OUT, SUM_IN, *other)
    landed(core_in, SUM_IN)
    pieces[...] = (acc[core] + core_in[...]).reshape(16, 16, 256)
    planes = [(dx, dy, 0) for dx in (2, 1, 3, 0) for dy in (2, 1, 3, 0) if dx or dy]
    for dx, dy, dz in planes:
        to = (me[0] + dx) % 4 * 4 + (me[1] + dy) % 4
        remote(pieces.at[to], plane_in.at[dom], SUM_OUT + 1, SUM_IN + 1, (dx, dy, 0), 0)
    plane_in[dom] = pieces[dom]
    landed(plane_in.at[pl.ds(0, 15)], SUM_IN + 1)
    line_in[me[2]] = jnp.sum(plane_in[...], axis=0)
    for step in (1, 2, 3):
        view = line_in.at[me[2]]
        remote(view, view, SUM_OUT + 2, SUM_IN + 2, along(2, step), 0)
    landed(line_in.at[pl.ds(0, 3)], SUM_IN + 2)
    final[core, dom] = jnp.sum(line_in[...], axis=0) * (1.0 / total_rows)
    view = final.at[core, dom]
    for n, (dx, dy, dz) in enumerate(planes):
        remote(view, view, SUM_OUT + 3, SUM_IN + 4 + n, (dx, dy, 0), 0)
    remote(view, view, SUM_OUT + 4, SUM_IN + 3, *other)
    for n, (dx, dy, dz) in enumerate(planes):
        view = final.at[core, (me[0] - dx) % 4 * 4 + (me[1] - dy) % 4]
        landed(view, SUM_IN + 4 + n)
        remote(view, view, SUM_OUT + 4, SUM_IN + 3, *other)
    landed(final.at[0], SUM_IN + 3)
    flipped = final[0].reshape(256, 256)
    lower = final[1].reshape(256, 256)
    gal_ref[...] = flipped.T
    lspg_ref[...] = lower
    lspg_ref[:128, 128:] = lower[128:, :128].T

    for h in range(2):
        for k in range(3):
            sent(two[h][k].at[pl.ds(0, 12)], in_id(h, 1, k))
            sent(tab[h][k].at[pl.ds(0, 112)], in_id(h, 2, k))
        sent(halo[h].at[pl.ds(0, 32)], HALO_OUT + h)
    sent(meta.at[pl.ds(0, 3), 0, 0], META_OUT)
    sent(meta.at[pl.ds(0, 3), :, 0], META_OUT + 1)
    sent(meta.at[:, :, pl.ds(0, 7)], META_OUT + 2)
    sent(core_in, SUM_OUT)
    sent(plane_in.at[pl.ds(0, 15)], SUM_OUT + 1)
    sent(line_in.at[pl.ds(0, 3)], SUM_OUT + 2)
    sent(final.at[0, pl.ds(0, 15)], SUM_OUT + 3)
    sent(final.at[0], SUM_OUT + 4)


def deliver(*refs):
    sources, results, sem = refs[:3], refs[3:6], refs[6]
    moves = []
    for n in range(PARTS):
        rows = pl.ds(n * (16 // PARTS), 16 // PARTS)
        moves.append((sources[2].at[rows], results[2].at[rows]))
    moves += [(sources[0], results[0]), (sources[1], results[1])]
    copies = [pltpu.make_async_copy(a, b, sem.at[n]) for n, (a, b) in enumerate(moves)]
    for copy in copies:
        copy.start()
    for copy in copies:
        copy.wait()


def body(basis, block_part, block_slot, face_slots, neighbors, jacobian):
    total_rows = 128 * basis.shape[0]
    blocks = basis.reshape(64, 128, 256)
    slabs = [(h, k) for h in range(2) for k in range(3)]
    scratch = [pltpu.VMEM((64, 128, 256), BF16), pltpu.VMEM((128, 3, 128, 128), BF16)]
    scratch += [pltpu.VMEM((4, 4, 8, SLABS[h][k], 128), BF16) for h, k in slabs]
    scratch += [pltpu.VMEM((16, 8, SLABS[h][k], 128), BF16) for h, k in slabs]
    scratch += [pltpu.VMEM((129, SLABS[h][k], 128), BF16) for h, k in slabs]
    scratch += [pltpu.VMEM((16, 128, 128), BF16)] * 2
    scratch += [pltpu.VMEM((33, 128, 128), BF16)] * 2
    scratch += [
        pltpu.VMEM((4, 4, 8, 1, 128), I32),
        pltpu.VMEM((8, 128), I32),
        pltpu.SMEM((8, 128), I32),
        pltpu.VMEM((2, 256, 256), F32),
        pltpu.VMEM((256, 256), F32),
        pltpu.VMEM((16, 16, 256), F32),
        pltpu.VMEM((16, 16, 256), F32),
        pltpu.VMEM((4, 16, 256), F32),
        pltpu.VMEM((2, 16, 16, 256), F32),
        pltpu.SemaphoreType.DMA((42,)),
        pltpu.SemaphoreType.DMA((28,)),
        pltpu.SemaphoreType.DMA((2,)),
        pltpu.SemaphoreType.DMA((1,)),
    ]
    smem = pl.BlockSpec(memory_space=pltpu.SMEM)
    vmem = pl.BlockSpec(memory_space=pltpu.VMEM)
    anywhere = pl.BlockSpec(memory_space=pl.ANY)
    galerkin, lspg, applied = pl.pallas_call(
        functools.partial(kernel, total_rows),
        out_shape=(
            pltpu.VMEM((256, 256), F32),
            pltpu.VMEM((256, 256), F32),
            pltpu.VMEM((16, 8, 128, 256), BF16),
        ),
        in_specs=[smem, smem, smem, smem, anywhere, anywhere],
        out_specs=(vmem, vmem, vmem),
        scratch_shapes=scratch,
        compiler_params=pltpu.CompilerParams(
            collective_id=0, has_side_effects=True, vmem_limit_bytes=54 * 2**20
        ),
        cost_estimate=pl.CostEstimate(
            flops=7_500_000_000, bytes_accessed=25_000_000, transcendentals=0
        ),
        name="regroup_apply_reduce",
    )(block_part, block_slot, face_slots, neighbors.T, blocks, jacobian)
    galerkin, lspg, applied = pl.pallas_call(
        deliver,
        out_shape=(
            jax.ShapeDtypeStruct((256, 256), F32),
            jax.ShapeDtypeStruct((256, 256), F32),
            jax.ShapeDtypeStruct((16, 8, 128, 256), BF16),
        ),
        in_specs=[vmem, vmem, vmem],
        out_specs=(anywhere, anywhere, anywhere),
        scratch_shapes=[pltpu.SemaphoreType.DMA((PARTS + 2,))],
        compiler_params=pltpu.CompilerParams(vmem_limit_bytes=16 * 2**20),
        cost_estimate=pl.CostEstimate(flops=0, bytes_accessed=17_800_000, transcendentals=0),
        name="deliver",
    )(galerkin, lspg, applied)
    return galerkin, lspg, applied.reshape(16384, 256)


def solution(mesh):
    in_specs = (
        P(("dom", "sub"), None),
        P(("dom", "sub")),
        P(("dom", "sub")),
        P(("dom", "sub"), None),
        P(("dom", "sub"), None),
        P(("dom", "sub"), None, None, None),
    )
    out_specs = (P(), P(), P(("dom", "sub"), None))
    return jax.shard_map(body, mesh=mesh, in_specs=in_specs, out_specs=out_specs, check_vma=False)
```

```python
import functools

import jax
import jax.numpy as jnp
from jax import lax
from jax.experimental import pallas as pl
from jax.experimental.pallas import tpu as pltpu
from jax.sharding import PartitionSpec as P

MESH = pl.DeviceIdType.MESH
BF16 = jnp.bfloat16
F32 = jnp.float32
I32 = jnp.int32

SLABS = ((48, 48, 32), (48, 48, 32))
ORDERS = ((0, 1, 2), (1, 2, 0), (2, 0, 1))
FACES = 4
FAR = (2, 1, 3, 0)
PARTS = 4
BATCH = 32
BEFORE = 3
EARLY = ((1, 0), (3, 0), (1, 1), (3, 1))
LATE = ((2, 0), (2, 1), (0, 1), (0, 0))


def offsets(h):
    out, at = [], 0
    for rows in SLABS[h]:
        out.append(at)
        at += rows
    return out


def kernel(
    total_rows,
    part_ref,
    slot_ref,
    face_ref,
    near_ref,
    basis_hbm,
    jac_hbm,
    gal_ref,
    lspg_ref,
    out_ref,
    basis,
    jac,
    one0, one1, one2, one3, one4, one5,
    two0, two1, two2, two3, two4, two5,
    tab0, tab1, tab2, tab3, tab4, tab5,
    face_out0, face_out1,
    halo0, halo1,
    meta,
    ints_v,
    ints_s,
    acc,
    core_in,
    pieces,
    cube_in,
    final,
    in_sem,
    out_sem,
    move_sem,
    local_sem,
):
    one = ((one0, one1, one2), (one3, one4, one5))
    two = ((two0, two1, two2), (two3, two4, two5))
    tab = ((tab0, tab1, tab2), (tab3, tab4, tab5))
    face_out = (face_out0, face_out1)
    halo = (halo0, halo1)

    dom = lax.axis_index("dom")
    sub = lax.axis_index("sub")
    me = (dom // 4, dom % 4, sub // 2)
    core = sub % 2
    rank = dom * 8 + sub

    def device(shift, flip):
        x, y, z = [(a + b) % 4 for a, b in zip(me, shift)]
        return (x * 4 + y, z * 2 + (core + flip) % 2)

    def along(dim, step):
        shift = [0, 0, 0]
        shift[dim] = step
        return tuple(shift)

    def remote(src, dst, s_sem, r_sem, shift, flip):
        pltpu.make_async_remote_copy(
            src, dst, out_sem.at[s_sem], in_sem.at[r_sem],
            device_id=device(shift, flip), device_id_type=MESH,
        ).start()

    def local(src, dst, r_sem):
        pltpu.make_async_copy(src, dst, in_sem.at[r_sem]).start()

    def landed(view, r_sem):
        pltpu.make_async_copy(view, view, in_sem.at[r_sem]).wait()

    def sent(view, s_sem):
        pltpu.make_async_copy(view, view, out_sem.at[s_sem]).wait()

    basis_copy = pltpu.make_async_copy(basis_hbm, basis, move_sem.at[0])
    basis_copy.start()
    jac_copy = pltpu.make_async_copy(jac_hbm, jac, move_sem.at[1])

    peers = [((0, 0, 0), 1)]
    for dim in range(3):
        for step in (1, 2, 3):
            peers += [(along(dim, step), 0), (along(dim, step), 1)]
    cube = [(dx, dy, dz) for dx in FAR for dy in FAR for dz in FAR if dx or dy or dz]
    peers += [(shift, 0) for shift in cube if (shift, 0) not in peers]
    barrier = pltpu.get_barrier_semaphore()
    for shift, flip in peers:
        pl.semaphore_signal(barrier, inc=1, device_id=device(shift, flip), device_id_type=MESH)

    lanes = lax.broadcasted_iota(I32, (1, 128), 1)

    def pick(b, carry):
        index, slot = carry
        hit = lanes == part_ref[b]
        return jnp.where(hit, b, index), jnp.where(hit, slot_ref[b], slot)

    index_row, slot_row = lax.fori_loop(
        0, 64, pick, (jnp.zeros((1, 128), I32), jnp.full((1, 128), -1, I32)), unroll=8
    )
    ints_v[0:1, :] = index_row
    mine = sub
    meta[me[0], me[1], mine] = slot_row
    ints_copy = pltpu.make_async_copy(ints_v, ints_s, local_sem.at[0])
    ints_copy.start()
    for h in range(2):
        for k in range(3):
            tab[h][k][128] = jnp.zeros(tab[h][k].shape[1:], BF16)
        halo[h][32] = jnp.zeros(halo[h].shape[1:], BF16)
    ints_copy.wait()
    basis_copy.wait()
    jac_copy.start()

    def gather(h):
        base = offsets(h)

        def one_block(p, carry):
            block = basis[ints_s[0, p], :, h * 128:(h + 1) * 128]
            to = (p // 32, (p // 8) % 4, (p // 2) % 4)
            for k, (d1, d2, d3) in enumerate(ORDERS):
                rows = SLABS[h][k]
                out_ref[to[d1] * 4 + to[d2], to[d3] * 2 + p % 2, base[k]:base[k] + rows,
                        h * 128:(h + 1) * 128] = block[base[k]:base[k] + rows]
            return carry

        lax.fori_loop(0, 128, one_block, 0, unroll=4)

    def in_id(h, stage, k):
        return (h * 3 + stage) * 3 + k

    def stage1(h, k):
        d1, d2, d3 = ORDERS[k]
        for step in (1, 2, 3, 0):
            to = (me[d1] + step) % 4
            src = out_ref.at[
                pl.ds(to * 4, 4), :, pl.ds(offsets(h)[k], SLABS[h][k]), pl.ds(h * 128, 128)]
            dst = one[h][k].at[me[d1]]
            if step:
                remote(src, dst, in_id(h, 0, k), in_id(h, 0, k), along(d1, step), 0)
            else:
                local(src, dst, in_id(h, 0, k))

    def stage2(h, k):
        d1, d2, d3 = ORDERS[k]
        for step in (1, 2, 3, 0):
            to = (me[d2] + step) % 4
            src = one[h][k].at[:, to]
            dst = two[h][k].at[pl.ds(me[d2] * 4, 4)]
            if step:
                remote(src, dst, in_id(h, 1, k), in_id(h, 1, k), along(d2, step), 0)
            else:
                local(src, dst, in_id(h, 1, k))

    def stage3(h, k, moves):
        d1, d2, d3 = ORDERS[k]
        dst = tab[h][k].at[pl.ds((me[d3] * 2 + core) * 16, 16)]
        for step, flip in moves:
            to = (me[d3] + step) % 4 * 2 + (core + flip) % 2
            src = two[h][k].at[:, to]
            if step or flip:
                remote(src, dst, in_id(h, 2, k), in_id(h, 2, k), along(d3, step), flip)
            else:
                local(src, dst, in_id(h, 2, k))

    gather(0)
    pl.semaphore_wait(barrier, len(peers))

    META_IN, META_OUT = 18, 18
    for step in (1, 2, 3):
        view = meta.at[me[0], me[1], mine]
        remote(view, view, META_OUT, META_IN, along(0, step), 0)

    for k in (1, 0, 2):
        stage1(0, k)
    gather(1)
    for k in (1, 0, 2):
        stage1(1, k)
    for h in range(2):
        for k in range(3):
            landed(one[h][k], in_id(h, 0, k))
            stage2(h, k)
    landed(meta.at[pl.ds(0, 3), 0, 0], META_IN)
    for step in (1, 2, 3):
        view = meta.at[:, me[1], mine]
        remote(view, view, META_OUT + 1, META_IN + 1, along(1, step), 0)
    for k in (2, 0, 1):
        landed(two[0][k], in_id(0, 1, k))
        stage3(0, k, EARLY + LATE)
    landed(meta.at[pl.ds(0, 3), :, 0], META_IN + 1)
    for step in (0, 1, 2, 3):
        for flip in (0, 1):
            if step or flip:
                view = meta.at[:, :, mine]
                remote(view, view, META_OUT + 2, META_IN + 2, along(2, step), flip)
    for k in (2, 0, 1):
        landed(two[1][k], in_id(1, 1, k))
        stage3(1, k, EARLY)

    landed(meta.at[:, :, pl.ds(0, 7)], META_IN + 2)
    arrived = meta[...].reshape(128, 1, 128)
    mine_only = lax.broadcasted_iota(I32, (128, 1, 128), 2) == rank
    slot_of = jnp.sum(jnp.where(mine_only, arrived, 0), axis=2, keepdims=True)
    hit = slot_of == lax.broadcasted_iota(I32, (128, 1, 128), 2)
    source = lax.broadcasted_iota(I32, (128, 1, 128), 0)
    from_ = (source // 32, (source // 8) % 4, (source // 2) % 4)
    for k, (d1, d2, d3) in enumerate(ORDERS):
        place = (from_[d3] * 2 + source % 2) * 16 + from_[d2] * 4 + from_[d1]
        ints_v[1 + k:2 + k, :] = jnp.max(jnp.where(hit, place, 0), axis=0)
    ints_v[4:5, :] = jnp.max(jnp.where(hit, 1, 0), axis=0)
    ints_copy = pltpu.make_async_copy(ints_v, ints_s, local_sem.at[0])
    ints_copy.start()
    ints_copy.wait()

    def table(h, slot):
        return jnp.concatenate([tab[h][k][ints_s[1 + k, slot]] for k in range(3)], axis=0)

    def entry(h, index):
        away = index >= 128
        slot = jnp.minimum(index, 127)
        slabs = [
            tab[h][k][jnp.where(away, 128, ints_s[1 + k, slot])] for k in range(3)
        ]
        near = jnp.concatenate(slabs, axis=0)
        return near + halo[h][jnp.where(away, index - 128, 32)]

    HALO_IN, HALO_OUT = 21, 21

    def send_faces(h):
        for k in range(3):
            landed(tab[h][k].at[pl.ds(0, 128)], in_id(h, 2, k))

        def one_face(e, carry):
            face_out[h][e] = table(h, face_ref[e // FACES, e % FACES])
            return carry

        lax.fori_loop(0, 4 * FACES, one_face, 0, unroll=2)
        dom_up = (((dom + 1) % 16), sub)
        dom_down = (((dom + 15) % 16), sub)
        sub_up = (dom, (sub + 1) % 8)
        sub_down = (dom, (sub + 7) % 8)
        moves = (
            (8, 8, 0, dom_up),
            (0, 8, 8, dom_down),
            (4, 4, 16, sub_up),
            (12, 4, 20, sub_up),
            (0, 4, 24, sub_down),
            (8, 4, 28, sub_down),
        )
        for src, count, dst, to in moves:
            pltpu.make_async_remote_copy(
                face_out[h].at[pl.ds(src, count)], halo[h].at[pl.ds(dst, count)],
                out_sem.at[HALO_OUT + h], in_sem.at[HALO_IN + h],
                device_id=to, device_id_type=MESH,
            ).start()

    contract = (((0,), (0,)), ((), ()))

    def tables(h, first):
        return jnp.concatenate([table(h, first + e) for e in range(BATCH)], axis=0)

    def applied(h, g):
        per = BATCH // 8
        rows = out_ref[pl.ds(g * per, per), :, :, h * 128:(h + 1) * 128]
        return rows.reshape(BATCH * 128, 128)

    def apply(h, low, high):
        def some_slots(g, carry):
            done = []
            for e in range(BATCH):
                s = g * BATCH + e
                right = jnp.concatenate(
                    [table(h, s), entry(h, near_ref[1, s]), entry(h, near_ref[2, s])], axis=0)
                left = jnp.concatenate([jac[s, 0], jac[s, 1], jac[s, 2]], axis=1)
                product = jnp.dot(left, right, preferred_element_type=F32)
                rows = (product * ints_s[4, s].astype(F32)).astype(BF16)
                out_ref[s // 8, s % 8, :, h * 128:(h + 1) * 128] = rows
                done.append(rows)
            rows = jnp.concatenate(done, axis=0)
            first = g * BATCH
            if h == 0:
                right = jnp.concatenate([tables(0, first), rows], axis=1)
                gram = lax.dot_general(rows, right, contract, preferred_element_type=F32)
                acc[0, 0, :128] += gram[:, :128]
                acc[1, 0, :128] += gram[:, 128:]
            else:
                right = jnp.concatenate(
                    [tables(0, first), tables(1, first), applied(0, g), rows], axis=1)
                gram = lax.dot_general(rows, right, contract, preferred_element_type=F32)
                for n in range(4):
                    acc[n // 2, n % 2, 128:] += gram[:, n * 128:(n + 1) * 128]
            return carry

        lax.fori_loop(low, high, some_slots, 0)

    def gram_across():
        def some_slots(g, carry):
            acc[0, 1, :128] += lax.dot_general(
                applied(0, g), tables(1, g * BATCH), contract, preferred_element_type=F32)
            return carry

        lax.fori_loop(0, 128 // BATCH, some_slots, 0)

    acc[...] = jnp.zeros_like(acc)
    send_faces(0)
    for k in (2, 0, 1):
        stage3(1, k, LATE)
    for h in range(2):
        for k in range(3):
            sent(one[h][k].at[pl.ds(0, 3)], in_id(h, 0, k))
    jac_copy.wait()
    landed(halo[0].at[pl.ds(0, 32)], HALO_IN)
    apply(0, 0, BEFORE)
    send_faces(1)
    apply(0, BEFORE, 128 // BATCH)
    gram_across()
    landed(halo[1].at[pl.ds(0, 32)], HALO_IN + 1)
    apply(1, 0, 128 // BATCH)

    SUM_IN, SUM_OUT = 23, 23
    other = ((0, 0, 0), 1)
    remote(acc.at[1 - core], core_in, SUM_OUT, SUM_IN, *other)
    landed(core_in, SUM_IN)
    pieces[...] = (acc[core] + core_in[...]).reshape(64, 8, 128)
    chip = dom * 4 + me[2]
    for dx, dy, dz in cube:
        to = ((me[0] + dx) % 4 * 4 + (me[1] + dy) % 4) * 4 + (me[2] + dz) % 4
        remote(pieces.at[to], cube_in.at[chip], SUM_OUT + 1, SUM_IN + 1, (dx, dy, dz), 0)
    cube_in[chip] = pieces[chip]
    landed(cube_in.at[pl.ds(0, 63)], SUM_IN + 1)
    final[core, chip] = jnp.sum(cube_in[...], axis=0) * (1.0 / total_rows)
    view = final.at[core, chip]
    for shift in cube:
        remote(view, view, SUM_OUT + 2, SUM_IN + 2, shift, 0)
    landed(final.at[0, pl.ds(0, 63)], SUM_IN + 2)
    remote(final.at[core], final.at[core], SUM_OUT + 3, SUM_IN + 3, *other)
    landed(final.at[0], SUM_IN + 3)
    flipped = final[0].reshape(2, 256, 128)
    lower = final[1].reshape(2, 256, 128)
    gal_ref[:128, :] = flipped[0].T
    gal_ref[128:, :] = flipped[1].T
    lspg_ref[:, :128] = lower[0]
    lspg_ref[:128, 128:] = lower[0, 128:].T
    lspg_ref[128:, 128:] = lower[1, 128:]

    for h in range(2):
        for k in range(3):
            sent(two[h][k].at[pl.ds(0, 12)], in_id(h, 1, k))
            sent(tab[h][k].at[pl.ds(0, 112)], in_id(h, 2, k))
        sent(halo[h].at[pl.ds(0, 32)], HALO_OUT + h)
    sent(meta.at[pl.ds(0, 3), 0, 0], META_OUT)
    sent(meta.at[pl.ds(0, 3), :, 0], META_OUT + 1)
    sent(meta.at[:, :, pl.ds(0, 7)], META_OUT + 2)
    sent(core_in, SUM_OUT)
    sent(cube_in.at[pl.ds(0, 63)], SUM_OUT + 1)
    sent(final.at[0, pl.ds(0, 63)], SUM_OUT + 2)
    sent(final.at[0], SUM_OUT + 3)


def deliver(*refs):
    sources, results, sem = refs[:3], refs[3:6], refs[6]
    moves = []
    for n in range(PARTS):
        rows = pl.ds(n * (16 // PARTS), 16 // PARTS)
        moves.append((sources[2].at[rows], results[2].at[rows]))
    moves += [(sources[0], results[0]), (sources[1], results[1])]
    copies = [pltpu.make_async_copy(a, b, sem.at[n]) for n, (a, b) in enumerate(moves)]
    for copy in copies:
        copy.start()
    for copy in copies:
        copy.wait()


def body(basis, block_part, block_slot, face_slots, neighbors, jacobian):
    total_rows = 128 * basis.shape[0]
    blocks = basis.reshape(64, 128, 256)
    slabs = [(h, k) for h in range(2) for k in range(3)]
    scratch = [pltpu.VMEM((64, 128, 256), BF16), pltpu.VMEM((128, 3, 128, 128), BF16)]
    scratch += [pltpu.VMEM((4, 4, 8, SLABS[h][k], 128), BF16) for h, k in slabs]
    scratch += [pltpu.VMEM((16, 8, SLABS[h][k], 128), BF16) for h, k in slabs]
    scratch += [pltpu.VMEM((129, SLABS[h][k], 128), BF16) for h, k in slabs]
    scratch += [pltpu.VMEM((16, 128, 128), BF16)] * 2
    scratch += [pltpu.VMEM((33, 128, 128), BF16)] * 2
    scratch += [
        pltpu.VMEM((4, 4, 8, 1, 128), I32),
        pltpu.VMEM((8, 128), I32),
        pltpu.SMEM((8, 128), I32),
        pltpu.VMEM((2, 2, 256, 128), F32),
        pltpu.VMEM((2, 256, 128), F32),
        pltpu.VMEM((64, 8, 128), F32),
        pltpu.VMEM((64, 8, 128), F32),
        pltpu.VMEM((2, 64, 8, 128), F32),
        pltpu.SemaphoreType.DMA((28,)),
        pltpu.SemaphoreType.DMA((28,)),
        pltpu.SemaphoreType.DMA((2,)),
        pltpu.SemaphoreType.DMA((1,)),
    ]
    smem = pl.BlockSpec(memory_space=pltpu.SMEM)
    vmem = pl.BlockSpec(memory_space=pltpu.VMEM)
    anywhere = pl.BlockSpec(memory_space=pl.ANY)
    galerkin, lspg, applied = pl.pallas_call(
        functools.partial(kernel, total_rows),
        out_shape=(
            pltpu.VMEM((256, 256), F32),
            pltpu.VMEM((256, 256), F32),
            pltpu.VMEM((16, 8, 128, 256), BF16),
        ),
        in_specs=[smem, smem, smem, smem, anywhere, anywhere],
        out_specs=(vmem, vmem, vmem),
        scratch_shapes=scratch,
        compiler_params=pltpu.CompilerParams(
            collective_id=0, has_side_effects=True, vmem_limit_bytes=54 * 2**20
        ),
        cost_estimate=pl.CostEstimate(
            flops=7_500_000_000, bytes_accessed=25_000_000, transcendentals=0
        ),
        name="regroup_apply_reduce",
    )(block_part, block_slot, face_slots, neighbors.T, blocks, jacobian)
    galerkin, lspg, applied = pl.pallas_call(
        deliver,
        out_shape=(
            jax.ShapeDtypeStruct((256, 256), F32),
            jax.ShapeDtypeStruct((256, 256), F32),
            jax.ShapeDtypeStruct((16, 8, 128, 256), BF16),
        ),
        in_specs=[vmem, vmem, vmem],
        out_specs=(anywhere, anywhere, anywhere),
        scratch_shapes=[pltpu.SemaphoreType.DMA((PARTS + 2,))],
        compiler_params=pltpu.CompilerParams(vmem_limit_bytes=16 * 2**20),
        cost_estimate=pl.CostEstimate(flops=0, bytes_accessed=17_800_000, transcendentals=0),
        name="deliver",
    )(galerkin, lspg, applied)
    return galerkin, lspg, applied.reshape(16384, 256)


def solution(mesh):
    in_specs = (
        P(("dom", "sub"), None),
        P(("dom", "sub")),
        P(("dom", "sub")),
        P(("dom", "sub"), None),
        P(("dom", "sub"), None),
        P(("dom", "sub"), None, None, None),
    )
    out_specs = (P(), P(), P(("dom", "sub"), None))
    return jax.shard_map(body, mesh=mesh, in_specs=in_specs, out_specs=out_specs, check_vma=False)
```
